32 devices in a mesh: rows: 16 (over z, y, core), rep: 2 (over x).
Axes of the slice: x: 2, y: 2, z: 4, core: 2. Of those that a mesh axis runs over, the one named last changes fastest.
Arguments:
- features: bfloat16 [16384, 256], P('rows'), may hold values from -6 to 6
- inv_sqrt_degree: bfloat16 [16384], P('rows'), may hold values from 0.25 to 1
- weight: bfloat16 [256, 256], replicated, may hold values from -0.375 to 0.375
- tile_vals: bfloat16 [16, 512, 128, 128], P('rows', 'rep'), may hold values from -0.0625 to 0.0625
- tile_row: int32 [16, 512], P('rows', 'rep'), may hold values from 0 to 7, as said below
- tile_col: int32 [16, 512], P('rows', 'rep'), may hold values from 0 to 63, as said below
- tile_count: int32 [16, 16], P('rows', 'rep'), may hold values from 0 to 64, as said below
- cotangent: bfloat16 [16384, 256], P('rows'), may hold values from -6 to 6
Outputs:
- activated: bfloat16 [16384, 256], P(('rows', 'rep'))
- weight_grad: float32 [256, 256], replicated
- feature_grad: bfloat16 [16384, 256], P(('rep', 'rows'))
The draws below stay inside these ranges and needn't reach their ends.
Inputs may be any that keep to these rules, and one draw needn't show every extreme that they name: `tile_count`: each count is at most 64; the 8 counts of row block i and columns r * 8 .. r * 8 + 7 sum to at most 256. Some pair holds exactly 64 tiles and some block row and replica exactly 256, in every draw. `tile_row`: the valid slots of a block row and replica are ordered by column block, and inside one block pair their positions are distinct. A valid slot counted for column block r * 8 + s has tile_col between s * 8 and s * 8 + 7.
All inputs are finite; a program needn't handle non-finite values.
Results may differ from the reference program's by a relative error of at most 0.015.
Values may be sent and summed in bfloat16 or wider, within the bound.
A program may use at most 128 MiB of HBM per device.

```python
import math
import jax
import jax.numpy as jnp
from jax import lax

F = 256
TS = 128
SECTIONS = 8
TB = 8
KB = 64
KT = 256
TILES = 512
NODES = 16384
N_ROWS = 16
N_REP = 2


def tile_layout(key):
    base = jax.random.fold_in(key, 11)
    k_heavy, k_raw, k_pick, k_perm, k_junk_row, k_junk_col = jax.random.split(base, 6)
    devices = N_ROWS * N_REP
    heavy = jax.random.randint(k_heavy, (N_ROWS, 1, 1), 1, 5)
    raw = jax.random.randint(k_raw, (N_ROWS, N_REP, SECTIONS), 0, KB + 1) * heavy // 4
    raw = raw.reshape(devices, SECTIONS).astype(jnp.int32)
    section_ids = jnp.arange(SECTIONS, dtype=jnp.int32)
    filled = jnp.clip(KT - section_ids * KB, 0, KB).astype(jnp.int32)
    chosen = jax.random.randint(k_pick, (), 0, devices)
    device_ids = jnp.arange(devices, dtype=jnp.int32)
    raw = jnp.where((device_ids == chosen)[:, None], filled[None, :], raw)
    totals = jnp.sum(raw, axis=1, keepdims=True)
    counts = (raw * KT // jnp.maximum(totals, KT)).astype(jnp.int32)
    ends = jnp.cumsum(counts, axis=1).astype(jnp.int32)
    starts = ends - counts
    slot_ids = jnp.arange(KT, dtype=jnp.int32)
    section_of = jnp.sum((slot_ids[None, :, None] >= ends[:, None, :]).astype(jnp.int32), axis=2)
    section_of = jnp.minimum(section_of, SECTIONS - 1).astype(jnp.int32)
    start_of = jnp.take_along_axis(starts, section_of, axis=1)
    within = jnp.clip(slot_ids[None, :] - start_of, 0, KB - 1)
    perm_keys = jax.random.split(k_perm, devices * SECTIONS)
    perms = jax.vmap(lambda one_key: jax.random.permutation(one_key, KB))(perm_keys)
    perms = perms.reshape(devices, SECTIONS, KB).astype(jnp.int32)
    position = perms[device_ids[:, None], section_of, within]
    valid = slot_ids[None, :] < ends[:, -1:]
    junk_row = jax.random.randint(k_junk_row, (devices, KT), 0, TB)
    junk_col = jax.random.randint(k_junk_col, (devices, KT), 0, SECTIONS * TB)
    rows = jnp.where(valid, position // TB, junk_row).astype(jnp.int32)
    cols = jnp.where(valid, section_of * TB + position % TB, junk_col).astype(jnp.int32)
    return (counts.reshape(N_ROWS, N_ROWS), rows.reshape(N_ROWS, TILES), cols.reshape(N_ROWS, TILES))


def draw_tile_count(key, part):
    return tile_layout(key)[0]


def draw_tile_row(key, part):
    return tile_layout(key)[1]


def draw_tile_col(key, part):
    return tile_layout(key)[2]


def levels(own_key, dims, shards, smallest, high):
    level = 1.0
    for axis_at, parts in shards:
        draws = jax.random.uniform(jax.random.fold_in(jax.random.fold_in(own_key, 6), axis_at), (parts,), jnp.float32, smallest / len(shards), high / len(shards))
        level = level * jnp.repeat(jnp.exp(draws), dims[axis_at] // parts).reshape((-1,) + (1,) * (len(dims) - 1 - axis_at))
    return level


def normal_values(stream_key, extent, scale, most, shards=(), held_as=jnp.bfloat16):
    result = jax.random.normal(stream_key, extent, jnp.float32) * scale
    if len(shards) > 0:
        result = levels(stream_key, extent, shards, -0.22, 0.18) * result
    return jnp.clip(result, min=-most, max=most).astype(held_as)


def setup_inputs(seed: int = 0) -> dict:
    key_list = jax.random.split(jax.random.key(seed), 9)
    return {
        "features": normal_values(key_list[0], (NODES, F), 1.0, 6.0, ((0, 16),)),
        "inv_sqrt_degree": jnp.clip(jnp.exp(math.log(1.0) - 1.3862944 * jax.random.uniform(key_list[1], (NODES,), jnp.float32) ** levels(key_list[1], (NODES,), ((0, 16),), -0.2, 0.2)), 0.25, 1.0).astype(jnp.bfloat16),
        "weight": normal_values(key_list[2], (F, F), F ** -0.5, 0.375),
        "tile_vals": normal_values(key_list[3], (N_ROWS, TILES, TS, TS), (N_REP * KT * TS // TB) ** -0.5, 0.0625, ((0, 16), (1, 2))),
        "tile_row": draw_tile_row(jax.random.fold_in(key_list[8], 71), 0),
        "tile_col": draw_tile_col(jax.random.fold_in(key_list[8], 71), 0),
        "tile_count": draw_tile_count(jax.random.fold_in(key_list[8], 71), 0),
        "cotangent": normal_values(key_list[7], (NODES, F), 1.0, 6.0, ((0, 16),)),
    }


def reference(features, inv_sqrt_degree, weight, tile_vals, tile_row, tile_col, tile_count, cotangent):
    devices = N_ROWS * N_REP
    nodes = features.shape[0]
    width = features.shape[1]
    tile = tile_vals.shape[-1]
    per_block = nodes // N_ROWS // tile
    slots = tile_vals.shape[1] // N_REP
    sections = N_ROWS // N_REP
    degree = inv_sqrt_degree.astype(jnp.float32)[:, None]
    scaled = (degree * features.astype(jnp.float32)).astype(jnp.bfloat16)
    values = tile_vals.reshape(devices, slots, tile, tile)
    rows_local = tile_row.reshape(devices, slots).astype(jnp.int32)
    cols_local = tile_col.reshape(devices, slots).astype(jnp.int32)
    totals = lax.optimization_barrier(jnp.sum(tile_count.reshape(devices, sections), axis=1)).astype(jnp.int32)
    device_ids = jnp.arange(devices, dtype=jnp.int32)
    out_tile = (device_ids // N_REP * per_block)[:, None] + rows_local
    in_tile = (device_ids % N_REP * (sections * per_block))[:, None] + cols_local
    keep = jnp.arange(slots, dtype=jnp.int32)[None, :] < totals[:, None]
    source_tiles = scaled.reshape(nodes // tile, tile, width)

    def forward_step(carry, item):
        vals, out_t, in_t, keep_d = item
        prod = jnp.einsum('kij,kjf->kif', vals.astype(jnp.float32), source_tiles[in_t].astype(jnp.float32))
        prod = jnp.where(keep_d[:, None, None], prod, jnp.float32(0.0))
        return (carry.at[out_t].add(prod), None)
    start = jnp.zeros((nodes // tile, tile, width), jnp.float32)
    summed, _ = lax.scan(forward_step, start, (values, out_tile, in_tile, keep))
    propagated = (degree * (summed.reshape(nodes, width) + scaled.astype(jnp.float32))).astype(jnp.bfloat16)
    preact = jnp.dot(propagated, weight, preferred_element_type=jnp.float32)
    gate = jax.nn.sigmoid(preact)
    activated = (preact * gate).astype(jnp.bfloat16)
    grad_pre = (cotangent.astype(jnp.float32) * gate * (1.0 + preact * (1.0 - gate))).astype(jnp.bfloat16)
    weight_grad = jnp.dot(propagated.T, grad_pre, preferred_element_type=jnp.float32) * jnp.float32(nodes ** (-0.5))
    back = (degree * jnp.dot(grad_pre, weight.T, preferred_element_type=jnp.float32)).astype(jnp.bfloat16)
    back_tiles = back.reshape(nodes // tile, tile, width)

    def backward_step(carry, item):
        vals, out_t, in_t, keep_d = item
        prod = jnp.einsum('kji,kjf->kif', vals.astype(jnp.float32), back_tiles[out_t].astype(jnp.float32))
        prod = jnp.where(keep_d[:, None, None], prod, jnp.float32(0.0))
        return (carry.at[in_t].add(prod), None)
    gathered, _ = lax.scan(backward_step, start, (values, out_tile, in_tile, keep))
    feature_grad = (degree * (gathered.reshape(nodes, width) + back.astype(jnp.float32))).astype(jnp.bfloat16)
    return (activated, weight_grad, feature_grad)
```

```python
import functools

import jax
import jax.numpy as jnp
from jax import lax
from jax.experimental import pallas as pl
from jax.experimental.pallas import tpu as pltpu
from jax.sharding import PartitionSpec as P

LIMIT = 48 * 2**20


def densify_kernel(per_block, starts, ends, rows, cols, vals_ref, dense_ref):
    section = pl.program_id(0)
    tile = vals_ref.shape[-1]
    dense_ref[...] = jnp.zeros_like(dense_ref)

    def place(slot, carry):
        row = pl.multiple_of(rows[slot] * tile, tile)
        col = pl.multiple_of((cols[slot] - section * per_block) * tile, tile)
        dense_ref[pl.ds(row, tile), pl.ds(col, tile)] = vals_ref[slot]
        return carry

    lax.fori_loop(starts[section], ends[section], place, 0)


def densify(values, rows, cols, starts, ends, per_block, sections):
    slots, tile, _ = values.shape
    block = per_block * tile
    return pl.pallas_call(
        functools.partial(densify_kernel, per_block),
        out_shape=jax.ShapeDtypeStruct((block, sections * block), values.dtype),
        grid_spec=pltpu.PrefetchScalarGridSpec(
            num_scalar_prefetch=4,
            grid=(sections,),
            in_specs=[pl.BlockSpec((slots, tile, tile), lambda s, *_: (0, 0, 0))],
            out_specs=pl.BlockSpec((block, block), lambda s, *_: (0, s)),
        ),
        compiler_params=pltpu.CompilerParams(vmem_limit_bytes=LIMIT),
        cost_estimate=pl.CostEstimate(
            flops=0, bytes_accessed=2 * (slots * tile * tile + block * sections * block), transcendentals=0
        ),
        name="densify",
    )(starts, ends, rows, cols, values)


def forward_kernel(dense_ref, source_ref, total_ref, sent_ref):
    section = pl.program_id(0)
    part = jnp.dot(dense_ref[...], source_ref[...], preferred_element_type=jnp.float32)

    @pl.when(section == 0)
    def _():
        total_ref[...] = part

    @pl.when(section > 0)
    def _():
        total_ref[...] += part

    @pl.when(section == pl.num_programs(0) - 1)
    def _():
        sent_ref[...] = total_ref[...].astype(sent_ref.dtype)


def forward(dense, source, sections):
    block, depth = dense.shape
    width = source.shape[-1]
    step = depth // sections
    return pl.pallas_call(
        forward_kernel,
        out_shape=(
            jax.ShapeDtypeStruct((block, width), jnp.float32),
            jax.ShapeDtypeStruct((block, width), jnp.bfloat16),
        ),
        grid=(sections,),
        in_specs=[
            pl.BlockSpec((block, step), lambda s: (0, s)),
            pl.BlockSpec((step, width), lambda s: (s, 0)),
        ],
        out_specs=(
            pl.BlockSpec((block, width), lambda s: (0, 0)),
            pl.BlockSpec((block, width), lambda s: (0, 0)),
        ),
        compiler_params=pltpu.CompilerParams(vmem_limit_bytes=LIMIT),
        cost_estimate=pl.CostEstimate(
            flops=2 * block * depth * width,
            bytes_accessed=2 * (block * depth + depth * width) + 6 * block * width,
            transcendentals=0,
        ),
        name="forward_product",
    )(dense, source)


def middle_kernel(
    share, factor, replica, own_ref, other_ref, feats_ref, deg_col_ref, deg_row_ref, weight_ref,
    cot_ref, act_ref, grad_ref, back_ref, prop_ref, pre_ref, full_ref,
):
    degree = deg_col_ref[...]
    scaled = (degree * feats_ref[...].astype(jnp.float32)).astype(jnp.bfloat16)
    summed = own_ref[...] + other_ref[...].astype(jnp.float32)
    propagated = (degree * (summed + scaled.astype(jnp.float32))).astype(jnp.bfloat16)
    weight = weight_ref[...]
    preact = jnp.dot(propagated, weight, preferred_element_type=jnp.float32)
    gate = jax.nn.sigmoid(preact)
    full_ref[...] = (preact * gate).astype(jnp.bfloat16)
    grad_pre = (cot_ref[...].astype(jnp.float32) * gate * (1.0 + preact * (1.0 - gate))).astype(
        jnp.bfloat16
    )
    prop_ref[...] = propagated
    pre_ref[...] = grad_pre
    spread = lax.dot_general(
        weight, grad_pre, (((1,), (1,)), ((), ())), preferred_element_type=jnp.float32
    )
    back_ref[...] = (deg_row_ref[...] * spread).astype(jnp.bfloat16)
    mine = pl.ds(pl.multiple_of(replica[0] * share, share), share)
    act_ref[...] = full_ref[mine, :]
    grad_ref[...] = factor * lax.dot_general(
        prop_ref[mine, :], pre_ref[mine, :], (((0,), (0,)), ((), ())),
        preferred_element_type=jnp.float32,
    )


def middle(replica, own, other, features, degree, weight, cotangent, share, factor):
    block, width = features.shape
    vmem = pl.BlockSpec(memory_space=pltpu.VMEM)
    return pl.pallas_call(
        functools.partial(middle_kernel, share, factor),
        out_shape=(
            jax.ShapeDtypeStruct((share, width), jnp.bfloat16),
            jax.ShapeDtypeStruct((width, width), jnp.float32),
            jax.ShapeDtypeStruct((width, block), jnp.bfloat16),
        ),
        in_specs=[pl.BlockSpec(memory_space=pltpu.SMEM)] + [vmem] * 7,
        out_specs=(vmem, vmem, vmem),
        scratch_shapes=[pltpu.VMEM((block, width), jnp.bfloat16)] * 3,
        compiler_params=pltpu.CompilerParams(vmem_limit_bytes=LIMIT),
        cost_estimate=pl.CostEstimate(
            flops=5 * block * width * width, bytes_accessed=16 * block * width, transcendentals=block * width
        ),
        name="middle",
    )(
        replica.reshape(1), own, other, features, degree.reshape(block, 1), degree.reshape(1, block),
        weight, cotangent,
    )


def backward_kernel(own_section, back_ref, dense_ref, out_ref):
    section = pl.program_id(0)
    back = back_ref[...]
    part = jnp.dot(back, dense_ref[...], preferred_element_type=jnp.float32)
    mine = (section == own_section[0]).astype(jnp.float32)
    part = (part + mine * back.astype(jnp.float32)).astype(out_ref.dtype)
    shares, _, share = out_ref.shape
    for piece in range(shares):
        out_ref[piece] = part[:, piece * share : (piece + 1) * share]


def backward(own_section, back, dense, sections, shares):
    width, block = back.shape
    depth = dense.shape[1]
    step = depth // sections
    share = step // shares
    return pl.pallas_call(
        backward_kernel,
        out_shape=jax.ShapeDtypeStruct((sections * shares, width, share), jnp.bfloat16),
        grid_spec=pltpu.PrefetchScalarGridSpec(
            num_scalar_prefetch=1,
            grid=(sections,),
            in_specs=[
                pl.BlockSpec((width, block), lambda s, *_: (0, 0)),
                pl.BlockSpec((block, step), lambda s, *_: (0, s)),
            ],
            out_specs=pl.BlockSpec((shares, width, share), lambda s, *_: (s, 0, 0)),
        ),
        compiler_params=pltpu.CompilerParams(vmem_limit_bytes=LIMIT),
        cost_estimate=pl.CostEstimate(
            flops=2 * block * depth * width,
            bytes_accessed=2 * (block * depth + depth * width + block * width),
            transcendentals=0,
        ),
        name="backward_product",
    )(own_section.reshape(1), back, dense)


def shards(features, inv_sqrt_degree, weight, tile_vals, tile_row, tile_col, tile_count, cotangent):
    rows_count = lax.axis_size("rows")
    rep_count = lax.axis_size("rep")
    sections = rows_count // rep_count
    replica = lax.axis_index("rep").astype(jnp.int32)
    block_row = lax.axis_index("rows").astype(jnp.int32)
    nodes_block, width = features.shape
    tile = tile_vals.shape[-1]
    per_block = nodes_block // tile
    share = nodes_block // rep_count
    counts = tile_count[0]
    ends = jnp.cumsum(counts).astype(jnp.int32)
    starts = ends - counts
    degree = inv_sqrt_degree.astype(jnp.float32)
    grad_factor = float(nodes_block * rows_count) ** (-0.5)

    route = []
    for row in range(rows_count):
        for rep in range(rep_count):
            goal_row = (row % sections) * rep_count + rep
            goal_rep = row // sections
            route.append((row * rep_count + rep, goal_row * rep_count + goal_rep))
    part_feats = lax.dynamic_slice_in_dim(features, replica * share, share, 0)
    part_degree = lax.dynamic_slice_in_dim(degree, replica * share, share, 0)
    part_scaled = (part_degree[:, None] * part_feats.astype(jnp.float32)).astype(jnp.bfloat16)
    placed = lax.ppermute(part_scaled, ("rows", "rep"), route)
    placed_degree = lax.ppermute(part_degree, ("rows", "rep"), route)
    source = lax.all_gather(placed, "rows", axis=0, tiled=True)

    dense = densify(tile_vals[0], tile_row[0], tile_col[0], starts, ends, per_block, sections)
    own, sent = forward(dense, source, sections)
    if rep_count == 2:
        other = lax.ppermute(sent, "rep", [(0, 1), (1, 0)])
    else:
        other = lax.psum(own, "rep") - own
    activated, local_grad, back = middle(
        replica, own, other, features, degree, weight, cotangent, share, grad_factor
    )
    weight_grad = lax.psum(local_grad, ("rows", "rep"))
    terms = backward(block_row - replica * sections, back, dense, sections, rep_count)
    gathered = lax.psum_scatter(terms, "rows", scatter_dimension=0, tiled=False)
    feature_grad = (placed_degree[:, None] * gathered.astype(jnp.float32).T).astype(jnp.bfloat16)
    return (activated, weight_grad, feature_grad)


def solution(mesh):
    placed = (
        P("rows", None),
        P("rows"),
        P(),
        P("rows", "rep", None, None),
        P("rows", "rep"),
        P("rows", "rep"),
        P("rows", "rep"),
        P("rows", None),
    )
    return jax.shard_map(
        shards,
        mesh=mesh,
        in_specs=placed,
        out_specs=(P(("rows", "rep"), None), P(), P(("rep", "rows"), None)),
        check_vma=False,
    )
```

```python
import functools

import jax
import jax.numpy as jnp
from jax import lax
from jax.experimental import pallas as pl
from jax.experimental.pallas import tpu as pltpu
from jax.sharding import PartitionSpec as P

LIMIT = 48 * 2**20


def densify_kernel(per_block, starts, ends, rows, cols, vals_ref, dense_ref):
    section = pl.program_id(0)
    tile = vals_ref.shape[-1]
    dense_ref[...] = jnp.zeros_like(dense_ref)

    def place(slot, carry):
        row = pl.multiple_of(rows[slot] * tile, tile)
        col = pl.multiple_of((cols[slot] - section * per_block) * tile, tile)
        dense_ref[pl.ds(row, tile), pl.ds(col, tile)] = vals_ref[slot]
        return carry

    lax.fori_loop(starts[section], ends[section], place, 0)


def densify(values, rows, cols, starts, ends, per_block, sections):
    slots, tile, _ = values.shape
    block = per_block * tile
    return pl.pallas_call(
        functools.partial(densify_kernel, per_block),
        out_shape=jax.ShapeDtypeStruct((block, sections * block), values.dtype),
        grid_spec=pltpu.PrefetchScalarGridSpec(
            num_scalar_prefetch=4,
            grid=(sections,),
            in_specs=[pl.BlockSpec((slots, tile, tile), lambda s, *_: (0, 0, 0))],
            out_specs=pl.BlockSpec((block, block), lambda s, *_: (0, s)),
        ),
        compiler_params=pltpu.CompilerParams(vmem_limit_bytes=LIMIT),
        cost_estimate=pl.CostEstimate(
            flops=0, bytes_accessed=2 * (slots * tile * tile + block * sections * block), transcendentals=0
        ),
        name="densify",
    )(starts, ends, rows, cols, values)


def forward_kernel(dense_ref, source_ref, total_ref, sent_ref):
    section = pl.program_id(0)
    part = jnp.dot(dense_ref[...], source_ref[...], preferred_element_type=jnp.float32)

    @pl.when(section == 0)
    def _():
        total_ref[...] = part

    @pl.when(section > 0)
    def _():
        total_ref[...] += part

    @pl.when(section == pl.num_programs(0) - 1)
    def _():
        sent_ref[...] = total_ref[...].astype(sent_ref.dtype)


def forward(dense, source, sections):
    block, depth = dense.shape
    width = source.shape[-1]
    step = depth // sections
    return pl.pallas_call(
        forward_kernel,
        out_shape=(
            jax.ShapeDtypeStruct((block, width), jnp.float32),
            jax.ShapeDtypeStruct((block, width), jnp.bfloat16),
        ),
        grid=(sections,),
        in_specs=[
            pl.BlockSpec((block, step), lambda s: (0, s)),
            pl.BlockSpec((step, width), lambda s: (s, 0)),
        ],
        out_specs=(
            pl.BlockSpec((block, width), lambda s: (0, 0)),
            pl.BlockSpec((block, width), lambda s: (0, 0)),
        ),
        compiler_params=pltpu.CompilerParams(vmem_limit_bytes=LIMIT),
        cost_estimate=pl.CostEstimate(
            flops=2 * block * depth * width,
            bytes_accessed=2 * (block * depth + depth * width) + 6 * block * width,
            transcendentals=0,
        ),
        name="forward_product",
    )(dense, source)


def middle_kernel(
    share, factor, replica, own_ref, other_ref, feats_ref, deg_col_ref, deg_row_ref, weight_ref,
    cot_ref, act_ref, grad_ref, back_ref, prop_ref, pre_ref, full_ref,
):
    degree = deg_col_ref[...]
    scaled = (degree * feats_ref[...].astype(jnp.float32)).astype(jnp.bfloat16)
    summed = own_ref[...] + other_ref[...].astype(jnp.float32)
    propagated = (degree * (summed + scaled.astype(jnp.float32))).astype(jnp.bfloat16)
    weight = weight_ref[...]
    preact = jnp.dot(propagated, weight, preferred_element_type=jnp.float32)
    gate = jax.nn.sigmoid(preact)
    full_ref[...] = (preact * gate).astype(jnp.bfloat16)
    grad_pre = (cot_ref[...].astype(jnp.float32) * gate * (1.0 + preact * (1.0 - gate))).astype(
        jnp.bfloat16
    )
    prop_ref[...] = propagated
    pre_ref[...] = grad_pre
    spread = lax.dot_general(
        weight, grad_pre, (((1,), (1,)), ((), ())), preferred_element_type=jnp.float32
    )
    back_ref[...] = (deg_row_ref[...] * spread).astype(jnp.bfloat16)
    mine = pl.ds(pl.multiple_of(replica[0] * share, share), share)
    act_ref[...] = full_ref[mine, :]
    grad_ref[...] = factor * lax.dot_general(
        prop_ref[mine, :], pre_ref[mine, :], (((0,), (0,)), ((), ())),
        preferred_element_type=jnp.float32,
    )


def middle(replica, own, other, features, degree, weight, cotangent, share, factor):
    block, width = features.shape
    vmem = pl.BlockSpec(memory_space=pltpu.VMEM)
    return pl.pallas_call(
        functools.partial(middle_kernel, share, factor),
        out_shape=(
            jax.ShapeDtypeStruct((share, width), jnp.bfloat16),
            jax.ShapeDtypeStruct((width, width), jnp.float32),
            jax.ShapeDtypeStruct((width, block), jnp.bfloat16),
        ),
        in_specs=[pl.BlockSpec(memory_space=pltpu.SMEM)] + [vmem] * 7,
        out_specs=(vmem, vmem, vmem),
        scratch_shapes=[pltpu.VMEM((block, width), jnp.bfloat16)] * 3,
        compiler_params=pltpu.CompilerParams(vmem_limit_bytes=LIMIT),
        cost_estimate=pl.CostEstimate(
            flops=5 * block * width * width, bytes_accessed=16 * block * width, transcendentals=block * width
        ),
        name="middle",
    )(
        replica.reshape(1), own, other, features, degree.reshape(block, 1), degree.reshape(1, block),
        weight, cotangent,
    )


def backward_kernel(own_section, back_ref, dense_ref, out_ref):
    section = pl.program_id(0)
    back = back_ref[...]
    part = jnp.dot(back, dense_ref[...], preferred_element_type=jnp.float32)
    mine = (section == own_section[0]).astype(jnp.float32)
    part = (part + mine * back.astype(jnp.float32)).astype(out_ref.dtype)
    shares, _, share = out_ref.shape
    for piece in range(shares):
        out_ref[piece] = part[:, piece * share : (piece + 1) * share]


def backward(own_section, back, dense, sections, shares):
    width, block = back.shape
    depth = dense.shape[1]
    step = depth // sections
    share = step // shares
    return pl.pallas_call(
        backward_kernel,
        out_shape=jax.ShapeDtypeStruct((sections * shares, width, share), jnp.bfloat16),
        grid_spec=pltpu.PrefetchScalarGridSpec(
            num_scalar_prefetch=1,
            grid=(sections,),
            in_specs=[
                pl.BlockSpec((width, block), lambda s, *_: (0, 0)),
                pl.BlockSpec((block, step), lambda s, *_: (0, s)),
            ],
            out_specs=pl.BlockSpec((shares, width, share), lambda s, *_: (s, 0, 0)),
        ),
        compiler_params=pltpu.CompilerParams(vmem_limit_bytes=LIMIT),
        cost_estimate=pl.CostEstimate(
            flops=2 * block * depth * width,
            bytes_accessed=2 * (block * depth + depth * width + block * width),
            transcendentals=0,
        ),
        name="backward_product",
    )(own_section.reshape(1), back, dense)


def sum_over_all(value, sizes):
    for axis, size in sizes:
        step = 1
        while step < size:
            value = value + lax.ppermute(value, axis, [(at, at ^ step) for at in range(size)])
            step *= 2
    return value


def shards(features, inv_sqrt_degree, weight, tile_vals, tile_row, tile_col, tile_count, cotangent):
    rows_count = lax.axis_size("rows")
    rep_count = lax.axis_size("rep")
    sections = rows_count // rep_count
    replica = lax.axis_index("rep").astype(jnp.int32)
    block_row = lax.axis_index("rows").astype(jnp.int32)
    nodes_block, width = features.shape
    tile = tile_vals.shape[-1]
    per_block = nodes_block // tile
    share = nodes_block // rep_count
    counts = tile_count[0]
    ends = jnp.cumsum(counts).astype(jnp.int32)
    starts = ends - counts
    degree = inv_sqrt_degree.astype(jnp.float32)
    grad_factor = float(nodes_block * rows_count) ** (-0.5)

    route = []
    for row in range(rows_count):
        for rep in range(rep_count):
            goal_row = (row % sections) * rep_count + rep
            goal_rep = row // sections
            route.append((row * rep_count + rep, goal_row * rep_count + goal_rep))
    part_feats = lax.dynamic_slice_in_dim(features, replica * share, share, 0)
    part_degree = lax.dynamic_slice_in_dim(degree, replica * share, share, 0)
    part_scaled = (part_degree[:, None] * part_feats.astype(jnp.float32)).astype(jnp.bfloat16)
    placed = lax.ppermute(part_scaled, ("rows", "rep"), route)
    placed_degree = lax.ppermute(part_degree, ("rows", "rep"), route)
    source = lax.all_gather(placed, "rows", axis=0, tiled=True)

    dense = densify(tile_vals[0], tile_row[0], tile_col[0], starts, ends, per_block, sections)
    own, sent = forward(dense, source, sections)
    if rep_count == 2:
        other = lax.ppermute(sent, "rep", [(0, 1), (1, 0)])
    else:
        other = lax.psum(own, "rep") - own
    activated, local_grad, back = middle(
        replica, own, other, features, degree, weight, cotangent, share, grad_factor
    )
    weight_grad = sum_over_all(local_grad, (("rep", rep_count), ("rows", rows_count)))
    terms = backward(block_row - replica * sections, back, dense, sections, rep_count)
    gathered = lax.psum_scatter(terms, "rows", scatter_dimension=0, tiled=False)
    feature_grad = (placed_degree[:, None] * gathered.astype(jnp.float32).T).astype(jnp.bfloat16)
    return (activated, weight_grad, feature_grad)


def solution(mesh):
    placed = (
        P("rows", None),
        P("rows"),
        P(),
        P("rows", "rep", None, None),
        P("rows", "rep"),
        P("rows", "rep"),
        P("rows", "rep"),
        P("rows", None),
    )
    return jax.shard_map(
        shards,
        mesh=mesh,
        in_specs=placed,
        out_specs=(P(("rows", "rep"), None), P(), P(("rep", "rows"), None)),
        check_vma=False,
    )
```

```python
import functools

import jax
import jax.numpy as jnp
from jax import lax
from jax.experimental import pallas as pl
from jax.experimental.pallas import tpu as pltpu
from jax.sharding import PartitionSpec as P

LIMIT = 48 * 2**20


def densify_kernel(per_block, starts, ends, rows, cols, vals_ref, dense_ref):
    section = pl.program_id(0)
    tile = vals_ref.shape[-1]
    dense_ref[...] = jnp.zeros_like(dense_ref)

    def place(slot, carry):
        row = pl.multiple_of(rows[slot] * tile, tile)
        col = pl.multiple_of((cols[slot] - section * per_block) * tile, tile)
        dense_ref[pl.ds(row, tile), pl.ds(col, tile)] = vals_ref[slot]
        return carry

    lax.fori_loop(starts[section], ends[section], place, 0)


def densify(values, rows, cols, starts, ends, per_block, sections):
    slots, tile, _ = values.shape
    block = per_block * tile
    return pl.pallas_call(
        functools.partial(densify_kernel, per_block),
        out_shape=jax.ShapeDtypeStruct((block, sections * block), values.dtype),
        grid_spec=pltpu.PrefetchScalarGridSpec(
            num_scalar_prefetch=4,
            grid=(sections,),
            in_specs=[pl.BlockSpec((slots, tile, tile), lambda s, *_: (0, 0, 0))],
            out_specs=pl.BlockSpec((block, block), lambda s, *_: (0, s)),
        ),
        compiler_params=pltpu.CompilerParams(vmem_limit_bytes=LIMIT),
        cost_estimate=pl.CostEstimate(
            flops=0, bytes_accessed=2 * (slots * tile * tile + block * sections * block), transcendentals=0
        ),
        name="densify",
    )(starts, ends, rows, cols, values)


def forward_kernel(dense_ref, source_ref, total_ref, sent_ref):
    section = pl.program_id(0)
    part = jnp.dot(dense_ref[...], source_ref[...], preferred_element_type=jnp.float32)

    @pl.when(section == 0)
    def _():
        total_ref[...] = part

    @pl.when(section > 0)
    def _():
        total_ref[...] += part

    @pl.when(section == pl.num_programs(0) - 1)
    def _():
        sent_ref[...] = total_ref[...].astype(sent_ref.dtype)


def forward(dense, source, sections, half):
    block, depth = dense.shape[0] // 2, dense.shape[1]
    width = source.shape[-1]
    step = depth // sections
    return pl.pallas_call(
        forward_kernel,
        out_shape=(
            jax.ShapeDtypeStruct((block, width), jnp.float32),
            jax.ShapeDtypeStruct((block, width), jnp.bfloat16),
        ),
        grid=(sections,),
        in_specs=[
            pl.BlockSpec((block, step), lambda s: (half, s)),
            pl.BlockSpec((step, width), lambda s: (s, 0)),
        ],
        out_specs=(
            pl.BlockSpec((block, width), lambda s: (0, 0)),
            pl.BlockSpec((block, width), lambda s: (0, 0)),
        ),
        compiler_params=pltpu.CompilerParams(vmem_limit_bytes=LIMIT),
        cost_estimate=pl.CostEstimate(
            flops=2 * block * depth * width,
            bytes_accessed=2 * (block * depth + depth * width) + 6 * block * width,
            transcendentals=0,
        ),
        name="forward_product_" + str(half),
    )(dense, source)


def middle_kernel(
    share, factor, replica, own0_ref, own1_ref, other0_ref, other1_ref, feats_ref, deg_col_ref, deg_row_ref, weight_ref,
    cot_ref, act_ref, grad_ref, back_ref, prop_ref, pre_ref, full_ref,
):
    degree = deg_col_ref[...]
    scaled = (degree * feats_ref[...].astype(jnp.float32)).astype(jnp.bfloat16)
    summed = jnp.concatenate(
        [
            own0_ref[...] + other0_ref[...].astype(jnp.float32),
            own1_ref[...] + other1_ref[...].astype(jnp.float32),
        ],
        axis=0,
    )
    propagated = (degree * (summed + scaled.astype(jnp.float32))).astype(jnp.bfloat16)
    weight = weight_ref[...]
    preact = jnp.dot(propagated, weight, preferred_element_type=jnp.float32)
    gate = jax.nn.sigmoid(preact)
    full_ref[...] = (preact * gate).astype(jnp.bfloat16)
    grad_pre = (cot_ref[...].astype(jnp.float32) * gate * (1.0 + preact * (1.0 - gate))).astype(
        jnp.bfloat16
    )
    prop_ref[...] = propagated
    pre_ref[...] = grad_pre
    spread = lax.dot_general(
        weight, grad_pre, (((1,), (1,)), ((), ())), preferred_element_type=jnp.float32
    )
    back_ref[...] = (deg_row_ref[...] * spread).astype(jnp.bfloat16)
    mine = pl.ds(pl.multiple_of(replica[0] * share, share), share)
    act_ref[...] = full_ref[mine, :]
    grad_ref[...] = factor * lax.dot_general(
        prop_ref[mine, :], pre_ref[mine, :], (((0,), (0,)), ((), ())),
        preferred_element_type=jnp.float32,
    )


def middle(replica, own, other, features, degree, weight, cotangent, share, factor):
    block, width = features.shape
    vmem = pl.BlockSpec(memory_space=pltpu.VMEM)
    return pl.pallas_call(
        functools.partial(middle_kernel, share, factor),
        out_shape=(
            jax.ShapeDtypeStruct((share, width), jnp.bfloat16),
            jax.ShapeDtypeStruct((width, width), jnp.float32),
            jax.ShapeDtypeStruct((width, block), jnp.bfloat16),
        ),
        in_specs=[pl.BlockSpec(memory_space=pltpu.SMEM)] + [vmem] * 9,
        out_specs=(vmem, vmem, vmem),
        scratch_shapes=[pltpu.VMEM((block, width), jnp.bfloat16)] * 3,
        compiler_params=pltpu.CompilerParams(vmem_limit_bytes=LIMIT),
        cost_estimate=pl.CostEstimate(
            flops=5 * block * width * width, bytes_accessed=16 * block * width, transcendentals=block * width
        ),
        name="middle",
    )(
        replica.reshape(1), *own, *other, features, degree.reshape(block, 1), degree.reshape(1, block),
        weight, cotangent,
    )


def backward_kernel(own_section, back_ref, dense_ref, out_ref):
    section = pl.program_id(0)
    back = back_ref[...]
    part = jnp.dot(back, dense_ref[...], preferred_element_type=jnp.float32)
    mine = (section == own_section[0]).astype(jnp.float32)
    part = (part + mine * back.astype(jnp.float32)).astype(out_ref.dtype)
    shares, _, share = out_ref.shape
    for piece in range(shares):
        out_ref[piece] = part[:, piece * share : (piece + 1) * share]


def backward(own_section, back, dense, sections, shares):
    width, block = back.shape
    depth = dense.shape[1]
    step = depth // sections
    share = step // shares
    return pl.pallas_call(
        backward_kernel,
        out_shape=jax.ShapeDtypeStruct((sections * shares, width, share), jnp.bfloat16),
        grid_spec=pltpu.PrefetchScalarGridSpec(
            num_scalar_prefetch=1,
            grid=(sections,),
            in_specs=[
                pl.BlockSpec((width, block), lambda s, *_: (0, 0)),
                pl.BlockSpec((block, step), lambda s, *_: (0, s)),
            ],
            out_specs=pl.BlockSpec((shares, width, share), lambda s, *_: (s, 0, 0)),
        ),
        compiler_params=pltpu.CompilerParams(vmem_limit_bytes=LIMIT),
        cost_estimate=pl.CostEstimate(
            flops=2 * block * depth * width,
            bytes_accessed=2 * (block * depth + depth * width + block * width),
            transcendentals=0,
        ),
        name="backward_product",
    )(own_section.reshape(1), back, dense)


def sum_over_all(value, sizes):
    for axis, size in sizes:
        step = 1
        while step < size:
            value = value + lax.ppermute(value, axis, [(at, at ^ step) for at in range(size)])
            step *= 2
    return value


def shards(features, inv_sqrt_degree, weight, tile_vals, tile_row, tile_col, tile_count, cotangent):
    rows_count = lax.axis_size("rows")
    rep_count = lax.axis_size("rep")
    sections = rows_count // rep_count
    replica = lax.axis_index("rep").astype(jnp.int32)
    block_row = lax.axis_index("rows").astype(jnp.int32)
    nodes_block, width = features.shape
    tile = tile_vals.shape[-1]
    per_block = nodes_block // tile
    share = nodes_block // rep_count
    counts = tile_count[0]
    ends = jnp.cumsum(counts).astype(jnp.int32)
    starts = ends - counts
    degree = inv_sqrt_degree.astype(jnp.float32)
    grad_factor = float(nodes_block * rows_count) ** (-0.5)

    route = []
    for row in range(rows_count):
        for rep in range(rep_count):
            goal_row = (row % sections) * rep_count + rep
            goal_rep = row // sections
            route.append((row * rep_count + rep, goal_row * rep_count + goal_rep))
    part_feats = lax.dynamic_slice_in_dim(features, replica * share, share, 0)
    part_degree = lax.dynamic_slice_in_dim(degree, replica * share, share, 0)
    part_scaled = (part_degree[:, None] * part_feats.astype(jnp.float32)).astype(jnp.bfloat16)
    placed = lax.ppermute(part_scaled, ("rows", "rep"), route)
    placed_degree = lax.ppermute(part_degree, ("rows", "rep"), route)
    source = lax.all_gather(placed, "rows", axis=0, tiled=True)

    dense = densify(tile_vals[0], tile_row[0], tile_col[0], starts, ends, per_block, sections)
    own, other = [], []
    for half in range(2):
        part, sent = forward(dense, source, sections, half)
        own.append(part)
        if rep_count == 2:
            other.append(lax.ppermute(sent, "rep", [(0, 1), (1, 0)]))
        else:
            other.append(lax.psum(part, "rep") - part)
    activated, local_grad, back = middle(
        replica, own, other, features, degree, weight, cotangent, share, grad_factor
    )
    weight_grad = sum_over_all(local_grad, (("rep", rep_count), ("rows", rows_count)))
    terms = backward(block_row - replica * sections, back, dense, sections, rep_count)
    gathered = lax.psum_scatter(terms, "rows", scatter_dimension=0, tiled=False)
    feature_grad = (placed_degree[:, None] * gathered.astype(jnp.float32).T).astype(jnp.bfloat16)
    return (activated, weight_grad, feature_grad)


def solution(mesh):
    placed = (
        P("rows", None),
        P("rows"),
        P(),
        P("rows", "rep", None, None),
        P("rows", "rep"),
        P("rows", "rep"),
        P("rows", "rep"),
        P("rows", None),
    )
    return jax.shard_map(
        shards,
        mesh=mesh,
        in_specs=placed,
        out_specs=(P(("rows", "rep"), None), P(), P(("rep", "rows"), None)),
        check_vma=False,
    )
```
